32 devices in a mesh: sec: 2 (over y), gx: 4 (over z), gy: 4 (over x, core).
Axes of the slice: x: 2, y: 2, z: 4, core: 2. Of those that a mesh axis runs over, the one named last changes fastest.
Arguments:
- ocean_velocity: float32 [2, 8, 256, 1024], P(None, None, 'gx', ('sec', 'gy')), may hold values from -6 to 6
- wind_stress: float32 [2, 256, 1024], P(None, 'gx', ('sec', 'gy')), may hold values from -6 to 6
- level_counts: int32 [256, 1024], P('gx', ('sec', 'gy')), may hold values from 1 to 8
- floe_position: float32 [4, 8, 2, 2048], P('gx', ('sec', 'gy')), may hold values from 0 to 4
- floe_velocity: float32 [4, 8, 2, 2048], P('gx', ('sec', 'gy')), may hold values from -3 to 3
- floe_radius: float32 [4, 8, 2048], P('gx', ('sec', 'gy')), may hold values from 0.5 to 1.5
- floe_mass: float32 [4, 8, 2048], P('gx', ('sec', 'gy')), may hold values from 0.5 to 5
- floe_polygon: float32 [4, 8, 32, 2048], P('gx', ('sec', 'gy')), may hold values from -2 to 2
- remap_cells: int32 [4, 8, 2048], P('gx', ('sec', 'gy')), may hold values from 0 to 32767, as said below
- contact_count: int32 [4, 8], P('gx', ('sec', 'gy')), may hold values from 8 to 64, as said below
- contact_list: int32 [4, 8, 3, 64], P('gx', ('sec', 'gy')), may hold values from 0 to 15, as said below
- move_index: int32 [4, 8, 8, 128], P('gx', ('sec', 'gy')), may hold values from 0 to 2047, as said below
- move_count: int32 [4, 8, 8], P('gx', ('sec', 'gy')), may hold values from 42 to 128, as said below
Outputs:
- ocean_next: float32 [2, 8, 256, 1024], P(None, None, 'gx', ('sec', 'gy'))
- floe_next: float32 [4, 8, 4, 2048], P('gx', ('sec', 'gy'))
- arrivals: float32 [4, 8, 8, 38, 128], P('gx', ('sec', 'gy'))
The draws below stay inside these ranges and needn't reach their ends.
Inputs may be any that keep to these rules, and one draw needn't show every extreme that they name: `contact_list`: row 0 of each slot names a block of the tile, 0 to 15; row 1 a source 0 to 8, 4 meaning the tile itself; row 2 a block of the source: 0 to 15 for source 4, else 0 to 3. Only the first contact_count slots count. `contact_count`: some tile uses all 64 slots in every draw. `move_index`: the floes named by one tile over all directions and slots are distinct. `move_count`: every tile fills all 128 slots towards at least one neighbour. `remap_cells`: Row-major index over the 256 rows and the tile's 128 columns. The floes of tile row i lie in grid rows i * 64 - 64 // 2 to i * 64 + 64 + 64 // 2 - 1 (within the grid), and every tile has floes in the first and the last row of that band.
All inputs are finite; a program needn't handle non-finite values.
Results may differ from the reference program's by a relative error of at most 0.0003.
Values sent between devices are 32-bit elements; how exact they have to be, the bound alone decides.
A program may use at most 64 MiB of HBM per device.

```python
import math
import jax
import jax.numpy as jnp
from jax import lax

CX = 64
CY = 128
LEV = 8
OSTEPS = 4
NB = 16
GHOST = 4
CMAX = 64
MIG = 128
NV = 16
FLOE_DEV = 2048
TILE_ROWS = 4
TILE_COLS = 8
NX = 256
NY = 1024


def draw_remap_cells(key, part):
    row_key, col_key = jax.random.split(jax.random.fold_in(key, 11))
    shape = (TILE_ROWS, TILE_COLS, FLOE_DEV)
    offsets = jax.random.randint(row_key, shape, 0, 2 * CX)
    base = jnp.arange(TILE_ROWS, dtype=jnp.int32)[:, None, None] * CX - CX // 2
    lowest = jnp.clip(base, 0, NX - 1)
    highest = jnp.clip(base + 2 * CX - 1, 0, NX - 1)
    rows_drawn = jnp.clip(base + offsets, 0, NX - 1)
    cols_drawn = jax.random.randint(col_key, shape, 0, CY)
    which = jnp.arange(FLOE_DEV, dtype=jnp.int32)[None, None, :]
    rows_drawn = jnp.where(which == 0, lowest, jnp.where(which == 1, highest, rows_drawn))
    cols_drawn = jnp.where(which == 0, 0, jnp.where(which == 1, CY - 1, cols_drawn))
    return (rows_drawn * CY + cols_drawn).astype(jnp.int32)


def draw_contact_count(key, part):
    first_key, second_key = jax.random.split(key)
    tiles = TILE_ROWS * TILE_COLS
    halvings = jax.random.randint(first_key, (tiles,), 0, 4)
    counts = jnp.right_shift(jnp.full((tiles,), CMAX, jnp.int32), halvings.astype(jnp.int32))
    busiest = jax.random.randint(second_key, (), 0, tiles)
    counts = jnp.where(jnp.arange(tiles) == busiest, CMAX, counts)
    return counts.reshape(TILE_ROWS, TILE_COLS).astype(jnp.int32)


def draw_contact_list(key, part):
    block_key, source_key, other_key = jax.random.split(key, 3)
    shape = (TILE_ROWS, TILE_COLS, CMAX)
    own_block = jax.random.randint(block_key, shape, 0, NB)
    picked = jax.random.randint(source_key, shape, 0, 16)
    shifted = picked - 8
    source = jnp.where(picked < 8, 4, shifted + (shifted >= 4).astype(jnp.int32))
    other = jax.random.randint(other_key, shape, 0, NB)
    other = jnp.where(source == 4, other, other % GHOST)
    return jnp.stack([own_block, source, other], axis=2).astype(jnp.int32)


def draw_move_index(key, part):
    keys = jax.random.split(key, TILE_ROWS * TILE_COLS)
    chosen = jax.vmap(lambda single: jax.random.permutation(single, FLOE_DEV)[:8 * MIG])(keys)
    return chosen.reshape(TILE_ROWS, TILE_COLS, 8, MIG).astype(jnp.int32)


def draw_move_count(key, part):
    first_key, second_key = jax.random.split(key)
    counts = jax.random.randint(first_key, (TILE_ROWS, TILE_COLS, 8), MIG // 3, MIG + 1)
    fullest = jax.random.randint(second_key, (TILE_ROWS, TILE_COLS, 1), 0, 8)
    counts = jnp.where(jnp.arange(8)[None, None, :] == fullest, MIG, counts)
    return counts.astype(jnp.int32)


def plant(drawn, rng, low, top_value):
    dims = drawn.shape
    place = [jax.random.randint(jax.random.fold_in(rng, axis), (), 0, dims[axis]) for axis in range(len(dims))]
    drawn = drawn.at[tuple(place)].set(low)
    longest = dims.index(max(dims))
    place[longest] = (place[longest] + 1) % dims[longest]
    return drawn.at[tuple(place)].set(top_value)


def steps_of(stream_key, shape, shards, smallest, high):
    def one(dim, parts):
        heights = jax.random.uniform(jax.random.fold_in(jax.random.fold_in(stream_key, 6), dim), (parts,), jnp.float32, smallest / len(shards), high / len(shards))
        return jnp.repeat(jnp.exp(heights), shape[dim] // parts).reshape((-1,) + (1,) * (len(shape) - dim - 1))

    level = one(*shards[0])
    for cut in shards[1:]:
        level = level * one(*cut)
    return level


def scatter_about(rng, extent, spread, most, cuts=(), kind=jnp.bfloat16):
    values = spread * jax.random.normal(rng, extent, jnp.float32)
    if cuts:
        values = values * steps_of(rng, extent, cuts, -0.22, 0.18)
    return jnp.clip(values, -most, most).astype(kind)


def setup_inputs(seed: int = 0) -> dict:
    arg_keys = jax.random.split(jax.random.key(seed), 14)
    ocean_velocity = scatter_about(arg_keys[0], (2, LEV, NX, NY), 1.0, 6.0, ((2, 4), (3, 8)), jnp.float32)
    wind_stress = scatter_about(arg_keys[1], (2, NX, NY), 1.0, 6.0, ((1, 4), (2, 8)), jnp.float32)
    level_counts = plant(jax.random.randint(arg_keys[2], (NX, NY), 1, LEV + 1), jax.random.fold_in(arg_keys[2], 1), 1, LEV).astype(jnp.int32)
    floe_position = jnp.clip(4.0 * jax.random.uniform(arg_keys[3], (TILE_ROWS, TILE_COLS, 2, FLOE_DEV), jnp.float32) ** steps_of(arg_keys[3], (TILE_ROWS, TILE_COLS, 2, FLOE_DEV), ((0, 4), (1, 8)), -0.2, 0.2), 0.0, 4.0)
    floe_velocity = scatter_about(arg_keys[4], (TILE_ROWS, TILE_COLS, 2, FLOE_DEV), 0.5, 3.0, ((0, 4), (1, 8)), jnp.float32)
    floe_radius = jnp.clip(0.5 + 1.0 * jax.random.uniform(arg_keys[5], (TILE_ROWS, TILE_COLS, FLOE_DEV), jnp.float32) ** steps_of(arg_keys[5], (TILE_ROWS, TILE_COLS, FLOE_DEV), ((0, 4), (1, 8)), -0.2, 0.2), 0.5, 1.5)
    floe_mass = jnp.clip(jnp.exp(math.log(5.0) - 2.3025851 * jax.random.uniform(arg_keys[6], (TILE_ROWS, TILE_COLS, FLOE_DEV), jnp.float32) ** steps_of(arg_keys[6], (TILE_ROWS, TILE_COLS, FLOE_DEV), ((0, 4), (1, 8)), -0.2, 0.2)), 0.5, 5.0)
    floe_polygon = scatter_about(arg_keys[7], (TILE_ROWS, TILE_COLS, 2 * NV, FLOE_DEV), 0.3, 2.0, ((0, 4), (1, 8)), jnp.float32)
    remap_cells = draw_remap_cells(jax.random.fold_in(arg_keys[13], 71), 0)
    contact_count = draw_contact_count(jax.random.fold_in(arg_keys[13], 71), 0)
    contact_list = draw_contact_list(jax.random.fold_in(arg_keys[13], 71), 0)
    move_index = draw_move_index(jax.random.fold_in(arg_keys[13], 71), 0)
    move_count = draw_move_count(jax.random.fold_in(arg_keys[13], 71), 0)
    return {"ocean_velocity": ocean_velocity, "wind_stress": wind_stress, "level_counts": level_counts, "floe_position": floe_position, "floe_velocity": floe_velocity, "floe_radius": floe_radius, "floe_mass": floe_mass, "floe_polygon": floe_polygon, "remap_cells": remap_cells, "contact_count": contact_count, "contact_list": contact_list, "move_index": move_index, "move_count": move_count}


SOFTEN = 0.1
STIFFNESS = 0.1
DAMPING = 0.05
VERT_MIX = 0.15
CORIOLIS = 0.1
SURFACE_GAIN = 0.25
WATER_DRAG = 0.1
AIR_GAIN = 0.2
ICE_STEP = 0.5
PLACES = (0, 1, 2, 3, 5, 6, 7, 8)

def ocean_substep(flow, padded, wet, wind):
    levels_here = flow.shape[1]
    lap = padded[:, :, :-2, 1:-1] + padded[:, :, 2:, 1:-1] + padded[:, :, 1:-1, :-2] + padded[:, :, 1:-1, 2:] - 4.0 * flow
    depth = jnp.arange(levels_here, dtype=jnp.float32)
    horizontal = (0.15 - 0.05 * depth / levels_here)[None, :, None, None]
    flux = VERT_MIX * (flow[:, 1:] - flow[:, :-1]) * wet[None, 1:]
    empty = jnp.zeros_like(flow[:, :1])
    vert = jnp.concatenate([flux, empty], axis=1) - jnp.concatenate([empty, flux], axis=1)
    turning = jnp.stack([CORIOLIS * flow[1], -CORIOLIS * flow[0]])
    surface = jnp.concatenate([SURFACE_GAIN * wind[:, None], jnp.zeros_like(flow[:, 1:])], axis=1)
    return (flow + horizontal * lap + vert + turning + surface) * wet[None]

def pair_forces(first, second):
    delta_x = first[:, 0, :, None] - second[:, 0, None, :]
    delta_y = first[:, 1, :, None] - second[:, 1, None, :]
    distance = jnp.sqrt(delta_x * delta_x + delta_y * delta_y + SOFTEN * SOFTEN)
    reach = first[:, 4, :, None] + second[:, 4, None, :]
    intersection = jnp.maximum(reach - distance, 0.0)
    reduced = first[:, 4, :, None] * second[:, 4, None, :] / reach
    normal_x = delta_x / distance
    normal_y = delta_y / distance
    closing = (first[:, 2, :, None] - second[:, 2, None, :]) * normal_x + (first[:, 3, :, None] - second[:, 3, None, :]) * normal_y
    magnitude = intersection * reduced * (STIFFNESS - DAMPING * closing)
    return jnp.stack([lax.optimization_barrier(jnp.sum(magnitude * normal_x, axis=2)), lax.optimization_barrier(jnp.sum(magnitude * normal_y, axis=2))], axis=1)

def block_table(own, ghosts):
    blocks = own.shape[1] // 128
    edge_blocks = ghosts.shape[2] // 128
    mine = own.reshape(5, blocks, 128).transpose(1, 0, 2)
    theirs = ghosts.reshape(8, 5, edge_blocks, 128).transpose(0, 2, 1, 3).reshape(8 * edge_blocks, 5, 128)
    return jnp.concatenate([mine, theirs], axis=0)

def contact_batch(table, lists, valid, blocks, edge_blocks):
    source = lists[1]
    neighbour = source - (source > 4).astype(jnp.int32)
    partner = jnp.where(source == 4, lists[2], blocks + neighbour * edge_blocks + lists[2])
    forces = pair_forces(table[lists[0]], table[partner])
    forces = jnp.where(valid[:, None, None], forces, 0.0)
    onehot = (lists[0][:, None] == jnp.arange(blocks, dtype=jnp.int32)[None, :]).astype(jnp.float32)
    return jnp.einsum('pn,pcf->ncf', onehot, forces, precision=lax.Precision.HIGHEST)

def tile_contacts(own, ghosts, lists, count):
    blocks = own.shape[1] // 128
    edge_blocks = ghosts.shape[2] // 128
    table = block_table(own, ghosts)
    slots = lists.shape[1]
    batch = math.gcd(slots, 32)
    grouped = lists.reshape(3, slots // batch, batch).transpose(1, 0, 2)
    starts = jnp.arange(slots // batch, dtype=jnp.int32) * batch

    def accumulate(total, item):
        group, start = item
        valid = start + jnp.arange(batch, dtype=jnp.int32) < count
        return (total + contact_batch(table, group, valid, blocks, edge_blocks), None)
    total, unused = lax.scan(accumulate, jnp.zeros((blocks, 2, 128), jnp.float32), (grouped, starts))
    return total.transpose(1, 0, 2).reshape(2, blocks * 128)

def reference(ocean_velocity, wind_stress, level_counts, floe_position, floe_velocity, floe_radius, floe_mass, floe_polygon, remap_cells, contact_count, contact_list, move_index, move_count):
    levels_here = ocean_velocity.shape[1]
    wet = (jnp.arange(levels_here, dtype=jnp.int32)[:, None, None] < level_counts[None]).astype(jnp.float32)
    flow = ocean_velocity * wet[None]
    for substep in range(OSTEPS):
        padded = jnp.pad(flow, ((0, 0), (0, 0), (1, 1), (1, 1)))
        flow = ocean_substep(flow, padded, wet, wind_stress)
    ocean_next = flow
    surface = jnp.stack([flow[0, 0], flow[1, 0], wind_stress[0], wind_stress[1]])
    tile_rows, tile_cols, floes = remap_cells.shape
    strip_rows = remap_cells // CY
    strip_cols = jnp.arange(tile_cols, dtype=jnp.int32)[None, :, None] * CY + remap_cells % CY
    sampled = jnp.moveaxis(surface[:, strip_rows, strip_cols], 0, 2)
    record = jnp.concatenate([floe_position, floe_velocity, floe_radius[:, :, None]], axis=2)
    edge = record[:, :, :, :GHOST * 128]
    padded_edge = jnp.pad(edge, ((1, 1), (1, 1), (0, 0), (0, 0)))
    ghosts = jnp.stack([padded_edge[p // 3:p // 3 + tile_rows, p % 3:p % 3 + tile_cols] for p in PLACES], axis=2)
    devices = tile_rows * tile_cols
    contact = lax.map(lambda item: tile_contacts(*item), (record.reshape(devices, 5, floes), ghosts.reshape(devices, 8, 5, GHOST * 128), contact_list.reshape(devices, 3, -1), contact_count.reshape(devices)))
    contact = contact.reshape(tile_rows, tile_cols, 2, floes)
    area = math.pi * floe_radius * floe_radius
    relative = sampled[:, :, 0:2] - floe_velocity
    speed = jnp.sqrt(lax.optimization_barrier(jnp.sum(relative * relative, axis=2, keepdims=True)))
    total = contact + area[:, :, None] * (WATER_DRAG * speed * relative + AIR_GAIN * sampled[:, :, 2:4])
    new_velocity = floe_velocity + ICE_STEP * total / floe_mass[:, :, None]
    new_position = floe_position + ICE_STEP * new_velocity
    floe_next = jnp.concatenate([new_position, new_velocity], axis=2)
    rows_all = jnp.concatenate([floe_next, floe_radius[:, :, None], floe_mass[:, :, None], floe_polygon], axis=2)
    width = rows_all.shape[2]
    slots = move_index.shape[3]
    chosen = move_index.reshape(tile_rows, tile_cols, 1, 8 * slots)
    taken = jnp.take_along_axis(rows_all, jnp.broadcast_to(chosen, (tile_rows, tile_cols, width, 8 * slots)), axis=3)
    taken = taken.reshape(tile_rows, tile_cols, width, 8, slots).transpose(0, 1, 3, 2, 4)
    valid = jnp.arange(slots, dtype=jnp.int32)[None, None, None, :] < move_count[:, :, :, None]
    outgoing = jnp.where(valid[:, :, :, None, :], taken, 0.0)
    padded_out = jnp.pad(outgoing, ((1, 1), (1, 1), (0, 0), (0, 0), (0, 0)))
    pieces = []
    for way in range(8):
        row_step = PLACES[way] // 3 - 1
        col_step = PLACES[way] % 3 - 1
        pieces.append(padded_out[1 - row_step:1 - row_step + tile_rows, 1 - col_step:1 - col_step + tile_cols, way])
    arrivals = jnp.stack(pieces, axis=2)
    return (ocean_next, floe_next, arrivals)
```

```python
import functools
import math

import jax
import jax.numpy as jnp
from jax import lax
from jax.experimental import pallas as pl
from jax.experimental.pallas import tpu as pltpu
from jax.sharding import PartitionSpec as P

OSTEPS = 4
GHOST = 4
SOFTEN = 0.1
STIFFNESS = 0.1
DAMPING = 0.05
VERT_MIX = 0.15
CORIOLIS = 0.1
SURFACE_GAIN = 0.25
WATER_DRAG = 0.1
AIR_GAIN = 0.2
ICE_STEP = 0.5
PLACES = (0, 1, 2, 3, 5, 6, 7, 8)
UP, LEFT, RIGHT, DOWN = 1, 3, 4, 6
MESH = pl.DeviceIdType.MESH
f32 = jnp.float32
UNROLL = 2


def lane_gather(values, lanes):
    return jnp.take_along_axis(values, lanes, axis=1, mode="promise_in_bounds")


def iota(shape, dim):
    return lax.broadcasted_iota(jnp.int32, shape, dim)


def kernel(
    ocean, wind, counts, pos, vel, rad, mass, poly, cells, ccount, clist, clist_v, mindex, mcount,
    ocean_out, floe_out, arrive_out,
    flow, cnt, wnd, halo_o, halo_c, pack, side, corner, edge72, own, gh, cols, forces,
    surf, late_s, early_s, early_r, next_s, next_r,
    sem_s, sem_r,
):
    levels, rows, width = ocean.shape[1], ocean.shape[2], ocean.shape[3]
    floes = pos.shape[1]
    blocks = floes // 128
    ext = rows + 8
    margin = rows // 2
    slots = clist.shape[1]
    n_gy = lax.axis_size("gy")
    n_rows, n_cols = lax.axis_size("gx"), lax.axis_size("sec") * n_gy
    row = lax.axis_index("gx")
    col = lax.axis_index("sec") * n_gy + lax.axis_index("gy")

    there, ids = [], []
    for way in range(8):
        dr, dc = PLACES[way] // 3 - 1, PLACES[way] % 3 - 1
        r, c = row + dr, col + dc
        there.append((r >= 0) & (r < n_rows) & (c >= 0) & (c < n_cols))
        ids.append((c // n_gy, r, c % n_gy))

    def copy(src, dst, number, way):
        return pltpu.make_async_remote_copy(
            src_ref=src, dst_ref=dst, send_sem=sem_s.at[number], recv_sem=sem_r.at[number],
            device_id=ids[way], device_id_type=MESH,
        )

    for ref in (halo_o, halo_c, side, corner, gh, early_r, next_r):
        ref[...] = jnp.zeros_like(ref)
    surf[:, 0:margin] = jnp.zeros((4, margin, width), f32)
    surf[:, margin + rows :] = jnp.zeros((4, margin, width), f32)

    barrier = pltpu.get_barrier_semaphore()
    for way in range(8):
        @pl.when(there[way])
        def _():
            pl.semaphore_signal(barrier, inc=1, device_id=ids[way], device_id_type=MESH)

    for b in range(blocks):
        at = slice(128 * b, 128 * b + 128)
        own[b, 0:2] = pos[:, at]
        own[b, 2:4] = vel[:, at]
        own[b, 4:5] = rad[:, at]
        own[b, 5:8] = jnp.zeros((3, 128), f32)
    lane = iota((rows, width), 1)
    group = lane // 8
    pack_flow = jnp.zeros((rows, width), f32)
    for c in range(2):
        for k in range(levels):
            n = c * levels + k
            pack_flow = jnp.where(group == n, pltpu.roll(ocean[c, k], (8 * n + 4) % width, 1), pack_flow)
    pack[0] = pack_flow
    countf = counts[...].astype(f32)
    aux = jnp.zeros((rows, width), f32)
    for c in range(2):
        n = c * levels
        aux = jnp.where(group == n, pltpu.roll(wind[c], (8 * n + 4) % width, 1), aux)
        aux = jnp.where(group == n + 1, pltpu.roll(countf, (8 * n + 12) % width, 1), aux)
    pack[1] = aux

    pl.semaphore_wait(barrier, sum(t.astype(jnp.int32) for t in there))

    halo = []
    strips = []
    for way in range(8):
        dr, dc = PLACES[way] // 3 - 1, PLACES[way] % 3 - 1
        first = 0 if dr < 0 else rows - 8
        if dr == 0:
            halo.append((way, copy(pack, side.at[(dc + 1) // 2], way, way)))
        else:
            part = pl.ds(first, 8)
            d = (dr + 1) // 2
            halo.append((way, copy(pack.at[:, part], corner.at[d, dc + 1], way, way)))
            if dc == 0:
                halo.append((way, copy(ocean.at[:, :, part], halo_o.at[d], 8 + d, way)))
                halo.append((way, copy(counts.at[part], halo_c.at[d], 10 + d, way)))
                src = pl.ds(0 if dr < 0 else rows - margin, margin)
                dst = pl.ds(rows + margin if dr < 0 else 0, margin)
                halo.append((way, copy(wind.at[:, src], surf.at[2:4, dst], 12 + d, way)))
                strips.append((way, copy(late_s.at[:, src], surf.at[0:2, dst], 14 + d, way)))
    records = [(w, copy(own.at[0:GHOST], gh.at[pl.ds((7 - w) * GHOST, GHOST)], 16 + w, w)) for w in range(8)]
    early = [(w, copy(early_s.at[w], early_r.at[w], 24 + w, w)) for w in range(8)]
    late = [(w, copy(next_s.at[w], next_r.at[w], 32 + w, w)) for w in range(8)]

    def start(copies):
        for way, c in copies:
            pl.when(there[way])(c.start)

    def landed(copies):
        for way, c in copies:
            pl.when(there[7 - way])(c.wait_recv)

    def sent(copies):
        for way, c in copies:
            pl.when(there[way])(c.wait_send)

    start(halo)
    start(records)

    lane8 = iota((8, 128), 1)

    def gather_early(w, carry):
        index = jnp.broadcast_to(mindex[pl.ds(w, 1)], (8, 128))
        block, lanes = index // 128, index % 128
        valid = lane8 < mcount[0, w]
        groups = [jnp.zeros((8, 128), f32) for _ in range(5)]
        for b in range(blocks):
            at = slice(128 * b, 128 * b + 128)
            hit = block == b
            for g in range(4):
                groups[g] = jnp.where(hit, lane_gather(poly[8 * g : 8 * g + 8, at], lanes), groups[g])
            rm = jnp.concatenate([rad[:, at], mass[:, at], jnp.zeros((6, 128), f32)], axis=0)
            groups[4] = jnp.where(hit, lane_gather(rm, lanes), groups[4])
        for g in range(5):
            early_s[w, 8 * g : 8 * g + 8] = jnp.where(valid, groups[g], 0.0)
        return carry

    lax.fori_loop(0, 8, gather_early, 0)
    start(early)

    def own_cols(b, carry):
        cols[b] = own[b].T
        return carry

    lax.fori_loop(0, blocks, own_cols, 0)

    landed(halo)
    sub8 = iota((8, width), 0)
    cnt[0:rows] = countf
    cnt[rows:] = jnp.where(sub8 < 4, halo_c[0], halo_c[1]).astype(f32)
    for c in range(2):
        wnd[c, 0:rows] = SURFACE_GAIN * wind[c]
        below, above = surf[2 + c, margin + rows : margin + rows + 8], surf[2 + c, margin - 8 : margin]
        wnd[c, rows:] = SURFACE_GAIN * jnp.where(sub8 < 4, below, above)
        surf[2 + c, margin : margin + rows] = wind[c]

    def fill(k, carry):
        wet = (cnt[...] > k.astype(f32)).astype(f32)
        for c in range(2):
            flow[c, k, 0:rows] = ocean[c, k] * wet[0:rows]
            flow[c, k, rows:] = jnp.where(sub8 < 4, halo_o[0, c, k], halo_o[1, c, k]) * wet[rows:]
        return carry

    lax.fori_loop(0, levels, fill, 0)

    lane72 = iota((ext, width), 1)
    inner = (lane72 % 8) < 4
    level72 = (lane72 // 8) % levels
    level_f = level72.astype(f32)

    def joined(part):
        return [
            jnp.concatenate([mid, jnp.where(sub8 < 4, corner[0, dc, part], corner[1, dc, part])], axis=0)
            for mid, dc in ((side[1, part], 2), (pack[part], 1), (side[0, part], 0))
        ]

    packed_aux, packed_flow = joined(1), joined(0)
    steer = []
    for which in range(2):
        mixed = [jnp.where(inner, p[which], p[which + 1]) for p in (packed_flow, packed_aux)]
        deep = jnp.where(level72 == 1, mixed[1], 0.0)
        for shift in (8, 16, 32):
            deep = deep + pltpu.roll(deep, shift, 1)
        wet = (deep > level_f).astype(f32)
        edge72[which, 0] = mixed[0] * wet
        edge72[which, 1] = wet
        edge72[which, 2] = jnp.where(level72 == 0, SURFACE_GAIN * mixed[1], 0.0)

    def substep(step, carry):
        def level(k, fluxes):
            after = jnp.minimum(k + 1, levels - 1)
            deep = cnt[...]
            wet = (deep > k.astype(f32)).astype(f32)
            wet_after = (deep > after.astype(f32)).astype(f32)
            h = 0.15 - 0.05 * k.astype(f32) / levels
            here = [flow[0, k], flow[1, k]]
            surface_on = jnp.where(k == 0, 1.0, 0.0)
            new_fluxes = []
            for c in range(2):
                x = here[c]
                at = 64 * c + 8 * k
                before = pltpu.roll(edge72[0, 0], 125 - at + jnp.where(at > 125, width, 0), 1)
                behind = pltpu.roll(edge72[1, 0], 123 - at, 1)
                left = jnp.where(lane72 == 0, before, pltpu.roll(x, 1, 1))
                right = jnp.where(lane72 == width - 1, behind, pltpu.roll(x, width - 1, 1))
                lap = pltpu.roll(x, 1, 0) + pltpu.roll(x, ext - 1, 0) + left + right - 4.0 * x
                flux = VERT_MIX * (flow[c, after] - x) * wet_after
                turn = CORIOLIS * here[1] if c == 0 else -CORIOLIS * here[0]
                new = x + h * lap + (flux - fluxes[c]) + turn + surface_on * wnd[c]
                flow[c, k] = new * wet
                new_fluxes.append(flux)
            return tuple(new_fluxes)

        nothing = jnp.zeros((ext, width), f32)
        lax.fori_loop(0, levels, level, (nothing, nothing))
        hp = 0.15 - 0.05 * level_f / levels
        turn_by = jnp.where(lane72 < 64, CORIOLIS, -CORIOLIS)
        for which in range(2):
            x, wet = edge72[which, 0], edge72[which, 1]
            lap = (
                pltpu.roll(x, 1, 0) + pltpu.roll(x, ext - 1, 0)
                + pltpu.roll(x, 1, 1) + pltpu.roll(x, width - 1, 1) - 4.0 * x
            )
            flux = VERT_MIX * (pltpu.roll(x, width - 8, 1) - x) * pltpu.roll(wet, width - 8, 1)
            flux = jnp.where(level72 < levels - 1, flux, 0.0)
            turn = turn_by * pltpu.roll(x, 64, 1)
            new = x + hp * lap + (flux - pltpu.roll(flux, 8, 1)) + turn + edge72[which, 2]
            edge72[which, 0] = new * wet
        return carry

    lax.fori_loop(0, OSTEPS, substep, 0)

    for c in range(2):
        late_s[c] = flow[c, 0, 0:rows]
    start(strips)
    for c in range(2):
        surf[c, margin : margin + rows] = late_s[c]

    def write(k, carry):
        for c in range(2):
            ocean_out[c, k] = flow[c, k, 0:rows]
        return carry

    lax.fori_loop(0, levels, write, 0)

    landed(records)

    def ghost_cols(b, carry):
        cols[blocks + b] = gh[b].T
        return carry

    lax.fori_loop(0, 8 * GHOST, ghost_cols, 0)

    def contact(t, carry):
        a, s, c = clist[0, t], clist[1, t], clist[2, t]
        neighbour = s - (s > 4).astype(jnp.int32)
        partner = jnp.where(s == 4, c, blocks + neighbour * GHOST + c)
        partner = jnp.clip(partner, 0, blocks + 8 * GHOST - 1)
        mine = own[a]
        other = cols[partner]
        step = 16
        xi, yi, ui, vi, ri = [jnp.broadcast_to(mine[f : f + 1], (step, 128)) for f in range(5)]
        sx = jnp.zeros((step, 128), f32)
        sy = jnp.zeros((step, 128), f32)
        for q in range(0, 128, step):
            xj, yj, uj, vj, rj = [
                jnp.broadcast_to(other[q : q + step, f : f + 1], (step, 128)) for f in range(5)
            ]
            dx, dy = xi - xj, yi - yj
            square = dx * dx + dy * dy + SOFTEN * SOFTEN
            inverse = lax.rsqrt(square)
            reach = ri + rj
            overlap = jnp.maximum(reach - square * inverse, 0.0)
            reduced = ri * rj / reach
            closing = ((ui - uj) * dx + (vi - vj) * dy) * inverse
            m = overlap * reduced * (STIFFNESS - DAMPING * closing) * inverse
            sx = sx + m * dx
            sy = sy + m * dy
        forces[0, pl.ds(t, 1)] = jnp.sum(sx, axis=0, keepdims=True)
        forces[1, pl.ds(t, 1)] = jnp.sum(sy, axis=0, keepdims=True)
        return carry

    lax.fori_loop(0, slots, contact, 0, unroll=UNROLL)
    takes = (iota((blocks, slots), 0) == clist_v[0:1]) & (iota((blocks, slots), 1) < ccount[0, 0])
    takes = takes.astype(f32)
    push = [
        jnp.dot(takes, forces[c], precision=lax.Precision.HIGHEST, preferred_element_type=f32)
        for c in range(2)
    ]

    landed(strips)
    pieces = []
    for n in range(4):
        turned = surf[n].T
        high = turned.astype(jnp.bfloat16)
        low = (turned - high.astype(f32)).astype(jnp.bfloat16)
        pieces.append(jnp.concatenate([high, low], axis=1))
    table = jnp.concatenate(pieces, axis=0)
    first_cell = (row * rows - margin) * width
    sub = iota((2 * rows, 128), 0)
    columns = iota((width, 128), 0)
    for b in range(blocks):
        at = slice(128 * b, 128 * b + 128)
        q = cells[:, at] - first_cell
        hit_row = (sub == q // width).astype(f32).astype(jnp.bfloat16)
        found = jnp.dot(table, jnp.concatenate([hit_row, hit_row], axis=0), preferred_element_type=f32)
        hit_col = columns == q % width
        su, sv, wx, wy = [
            jnp.sum(jnp.where(hit_col, found[width * n : width * n + width], 0.0), axis=0, keepdims=True)
            for n in range(4)
        ]
        r = rad[:, at]
        u, v = vel[0:1, at], vel[1:2, at]
        area = math.pi * r * r
        ru, rv = su - u, sv - v
        speed = jnp.sqrt(ru * ru + rv * rv)
        fx = push[0][b : b + 1] + area * (WATER_DRAG * speed * ru + AIR_GAIN * wx)
        fy = push[1][b : b + 1] + area * (WATER_DRAG * speed * rv + AIR_GAIN * wy)
        per_mass = ICE_STEP / mass[:, at]
        nu, nv = u + fx * per_mass, v + fy * per_mass
        floe_out[0:1, at] = pos[0:1, at] + ICE_STEP * nu
        floe_out[1:2, at] = pos[1:2, at] + ICE_STEP * nv
        floe_out[2:3, at] = nu
        floe_out[3:4, at] = nv

    def gather_late(w, carry):
        index = jnp.broadcast_to(mindex[pl.ds(w, 1)], (8, 128))
        block, lanes = index // 128, index % 128
        total = jnp.zeros((8, 128), f32)
        for b in range(blocks):
            values = floe_out[:, 128 * b : 128 * b + 128]
            values = jnp.concatenate([values, values], axis=0)
            total = jnp.where(block == b, lane_gather(values, lanes), total)
        next_s[w] = jnp.where(lane8 < mcount[0, w], total, 0.0)
        return carry

    lax.fori_loop(0, 8, gather_late, 0)
    start(late)
    landed(early)
    for w in range(8):
        arrive_out[w, 6:38] = early_r[w, 0:32]
        arrive_out[w, 4:6] = early_r[w, 32:34]
    landed(late)
    for w in range(8):
        arrive_out[w, 0:4] = next_r[w, 0:4]
    for copies in (halo, records, early, strips, late):
        sent(copies)


def shards(
    ocean_velocity, wind_stress, level_counts, floe_position, floe_velocity, floe_radius, floe_mass,
    floe_polygon, remap_cells, contact_count, contact_list, move_index, move_count,
):
    levels, rows, width = ocean_velocity.shape[1:]
    floes = floe_position.shape[-1]
    blocks = floes // 128
    slots = contact_list.shape[-1]
    ext = rows + 8
    lists = contact_list[0, 0]
    vmem = pl.BlockSpec(memory_space=pltpu.VMEM)
    smem = pl.BlockSpec(memory_space=pltpu.SMEM)
    fields = 2 + floe_polygon.shape[2] + 4
    flow, floe, arrivals = pl.pallas_call(
        kernel,
        out_shape=(
            jax.ShapeDtypeStruct(ocean_velocity.shape, f32),
            jax.ShapeDtypeStruct((4, floes), f32),
            jax.ShapeDtypeStruct((8, fields, 128), f32),
        ),
        in_specs=[vmem] * 9 + [smem, smem, vmem, vmem, smem],
        out_specs=(vmem, vmem, vmem),
        scratch_shapes=[
            pltpu.VMEM((2, levels, ext, width), f32),
            pltpu.VMEM((ext, width), f32),
            pltpu.VMEM((2, ext, width), f32),
            pltpu.VMEM((2, 2, levels, 8, width), f32),
            pltpu.VMEM((2, 8, width), jnp.int32),
            pltpu.VMEM((2, rows, width), f32),
            pltpu.VMEM((2, 2, rows, width), f32),
            pltpu.VMEM((2, 3, 2, 8, width), f32),
            pltpu.VMEM((2, 3, ext, width), f32),
            pltpu.VMEM((blocks, 8, 128), f32),
            pltpu.VMEM((8 * GHOST, 8, 128), f32),
            pltpu.VMEM((blocks + 8 * GHOST, 128, 8), f32),
            pltpu.VMEM((2, slots, 128), f32),
            pltpu.VMEM((4, 2 * rows, width), f32),
            pltpu.VMEM((2, rows, width), f32),
            pltpu.VMEM((8, 40, 128), f32),
            pltpu.VMEM((8, 40, 128), f32),
            pltpu.VMEM((8, 8, 128), f32),
            pltpu.VMEM((8, 8, 128), f32),
            pltpu.SemaphoreType.DMA((40,)),
            pltpu.SemaphoreType.DMA((40,)),
        ],
        compiler_params=pltpu.CompilerParams(
            collective_id=0, has_side_effects=True, vmem_limit_bytes=40 * 1024 * 1024
        ),
    )(
        ocean_velocity, wind_stress, level_counts, floe_position[0, 0], floe_velocity[0, 0],
        floe_radius[0], floe_mass[0], floe_polygon[0, 0], remap_cells[0], contact_count,
        lists, lists, move_index[0, 0], move_count[0],
    )
    return (flow, floe[None, None], arrivals[None, None])


def solution(mesh):
    tile = P("gx", ("sec", "gy"))
    return jax.shard_map(
        shards,
        mesh=mesh,
        in_specs=(
            P(None, None, "gx", ("sec", "gy")),
            P(None, "gx", ("sec", "gy")),
            tile, tile, tile, tile, tile, tile, tile, tile, tile, tile, tile,
        ),
        out_specs=(P(None, None, "gx", ("sec", "gy")), tile, tile),
        check_vma=False,
    )
```

```python
import functools
import math

import jax
import jax.numpy as jnp
from jax import lax
from jax.experimental import pallas as pl
from jax.experimental.pallas import tpu as pltpu
from jax.sharding import PartitionSpec as P

OSTEPS = 4
GHOST = 4
SOFTEN = 0.1
STIFFNESS = 0.1
DAMPING = 0.05
VERT_MIX = 0.15
CORIOLIS = 0.1
SURFACE_GAIN = 0.25
WATER_DRAG = 0.1
AIR_GAIN = 0.2
ICE_STEP = 0.5
PLACES = (0, 1, 2, 3, 5, 6, 7, 8)
UP, LEFT, RIGHT, DOWN = 1, 3, 4, 6
MESH = pl.DeviceIdType.MESH
f32 = jnp.float32
UNROLL = 4


def lane_gather(values, lanes):
    return jnp.take_along_axis(values, lanes, axis=1, mode="promise_in_bounds")


def iota(shape, dim):
    return lax.broadcasted_iota(jnp.int32, shape, dim)


def kernel(
    ocean_h, wind_h, counts_h, pos_h, vel_h, rad_h, mass_h, poly_h, cells_h,
    ccount, clist, clist_v, mindex, mcount,
    ocean_out, floe_out, arrive_out,
    flow, cnt, wnd, halo_o, halo_c, pack, side, corner, edge72, own, gh, cols, forces,
    surf, late_s, early_s, early_r, next_s, next_r,
    ocean, wind, counts, pos, vel, rad, mass, poly, cells,
    sem_s, sem_r, sem_i,
):
    loads = [
        pltpu.make_async_copy(src, dst, sem_i.at[n])
        for n, (src, dst) in enumerate((
            (ocean_h, ocean), (wind_h, wind), (counts_h, counts), (pos_h, pos), (vel_h, vel),
            (rad_h, rad), (poly_h, poly), (mass_h, mass), (cells_h, cells),
        ))
    ]
    for load in loads:
        load.start()
    levels, rows, width = ocean.shape[1], ocean.shape[2], ocean.shape[3]
    floes = pos.shape[1]
    blocks = floes // 128
    ext = rows + 8
    margin = rows // 2
    slots = clist.shape[1]
    n_gy = lax.axis_size("gy")
    n_rows, n_cols = lax.axis_size("gx"), lax.axis_size("sec") * n_gy
    row = lax.axis_index("gx")
    col = lax.axis_index("sec") * n_gy + lax.axis_index("gy")

    there, ids = [], []
    for way in range(8):
        dr, dc = PLACES[way] // 3 - 1, PLACES[way] % 3 - 1
        r, c = row + dr, col + dc
        there.append((r >= 0) & (r < n_rows) & (c >= 0) & (c < n_cols))
        ids.append((c // n_gy, r, c % n_gy))

    def copy(src, dst, number, way):
        return pltpu.make_async_remote_copy(
            src_ref=src, dst_ref=dst, send_sem=sem_s.at[number], recv_sem=sem_r.at[number],
            device_id=ids[way], device_id_type=MESH,
        )

    for ref in (halo_o, halo_c, side, corner, gh, early_r, next_r):
        ref[...] = jnp.zeros_like(ref)
    surf[:, 0:margin] = jnp.zeros((4, margin, width), f32)
    surf[:, margin + rows :] = jnp.zeros((4, margin, width), f32)

    barrier = pltpu.get_barrier_semaphore()
    for way in range(8):
        @pl.when(there[way])
        def _():
            pl.semaphore_signal(barrier, inc=1, device_id=ids[way], device_id_type=MESH)

    for load in loads[:6]:
        load.wait()
    for b in range(blocks):
        at = slice(128 * b, 128 * b + 128)
        own[b, 0:2] = pos[:, at]
        own[b, 2:4] = vel[:, at]
        own[b, 4:5] = rad[:, at]
        own[b, 5:8] = jnp.zeros((3, 128), f32)
    lane = iota((rows, width), 1)
    group = lane // 8
    pack_flow = jnp.zeros((rows, width), f32)
    for c in range(2):
        for k in range(levels):
            n = c * levels + k
            pack_flow = jnp.where(group == n, pltpu.roll(ocean[c, k], (8 * n + 4) % width, 1), pack_flow)
    pack[0] = pack_flow
    countf = counts[...].astype(f32)
    aux = jnp.zeros((rows, width), f32)
    for c in range(2):
        n = c * levels
        aux = jnp.where(group == n, pltpu.roll(wind[c], (8 * n + 4) % width, 1), aux)
        aux = jnp.where(group == n + 1, pltpu.roll(countf, (8 * n + 12) % width, 1), aux)
    pack[1] = aux

    pl.semaphore_wait(barrier, sum(t.astype(jnp.int32) for t in there))

    halo = []
    strips = []
    for way in range(8):
        dr, dc = PLACES[way] // 3 - 1, PLACES[way] % 3 - 1
        first = 0 if dr < 0 else rows - 8
        if dr == 0:
            halo.append((way, copy(pack, side.at[(dc + 1) // 2], way, way)))
        else:
            part = pl.ds(first, 8)
            d = (dr + 1) // 2
            halo.append((way, copy(pack.at[:, part], corner.at[d, dc + 1], way, way)))
            if dc == 0:
                halo.append((way, copy(ocean.at[:, :, part], halo_o.at[d], 8 + d, way)))
                halo.append((way, copy(counts.at[part], halo_c.at[d], 10 + d, way)))
                src = pl.ds(0 if dr < 0 else rows - margin, margin)
                dst = pl.ds(rows + margin if dr < 0 else 0, margin)
                halo.append((way, copy(wind.at[:, src], surf.at[2:4, dst], 12 + d, way)))
                strips.append((way, copy(late_s.at[:, src], surf.at[0:2, dst], 14 + d, way)))
    records = [(w, copy(own.at[0:GHOST], gh.at[pl.ds((7 - w) * GHOST, GHOST)], 16 + w, w)) for w in range(8)]
    early = [(w, copy(early_s.at[w], early_r.at[w], 24 + w, w)) for w in range(8)]
    late = [(w, copy(next_s.at[w], next_r.at[w], 32 + w, w)) for w in range(8)]

    def start(copies):
        for way, c in copies:
            pl.when(there[way])(c.start)

    def landed(copies):
        for way, c in copies:
            pl.when(there[7 - way])(c.wait_recv)

    def sent(copies):
        for way, c in copies:
            pl.when(there[way])(c.wait_send)

    start(records)
    start(halo)

    for load in loads[6:]:
        load.wait()
    lane8 = iota((8, 128), 1)

    def gather_early(w, carry):
        index = jnp.broadcast_to(mindex[pl.ds(w, 1)], (8, 128))
        block, lanes = index // 128, index % 128
        valid = lane8 < mcount[0, w]
        groups = [jnp.zeros((8, 128), f32) for _ in range(5)]
        for b in range(blocks):
            at = slice(128 * b, 128 * b + 128)
            hit = block == b
            for g in range(4):
                groups[g] = jnp.where(hit, lane_gather(poly[8 * g : 8 * g + 8, at], lanes), groups[g])
            rm = jnp.concatenate([rad[:, at], mass[:, at], jnp.zeros((6, 128), f32)], axis=0)
            groups[4] = jnp.where(hit, lane_gather(rm, lanes), groups[4])
        for g in range(5):
            early_s[w, 8 * g : 8 * g + 8] = jnp.where(valid, groups[g], 0.0)
        return carry

    lax.fori_loop(0, 8, gather_early, 0)
    start(early)

    def own_cols(b, carry):
        cols[b] = own[b].T
        return carry

    lax.fori_loop(0, blocks, own_cols, 0, unroll=8)

    landed(records)

    def ghost_cols(b, carry):
        cols[blocks + b] = gh[b].T
        return carry

    lax.fori_loop(0, 8 * GHOST, ghost_cols, 0, unroll=8)

    def contact(t, carry):
        a, s, c = clist[0, t], clist[1, t], clist[2, t]
        neighbour = s - (s > 4).astype(jnp.int32)
        partner = jnp.where(s == 4, c, blocks + neighbour * GHOST + c)
        partner = jnp.clip(partner, 0, blocks + 8 * GHOST - 1)
        mine = own[a]
        other = cols[partner]
        step = 16
        xi, yi, ui, vi, ri = [jnp.broadcast_to(mine[f : f + 1], (step, 128)) for f in range(5)]
        sx = jnp.zeros((step, 128), f32)
        sy = jnp.zeros((step, 128), f32)
        for q in range(0, 128, step):
            xj, yj, uj, vj, rj = [
                jnp.broadcast_to(other[q : q + step, f : f + 1], (step, 128)) for f in range(5)
            ]
            dx, dy = xi - xj, yi - yj
            square = dx * dx + dy * dy + SOFTEN * SOFTEN
            inverse = lax.rsqrt(square)
            reach = ri + rj
            overlap = jnp.maximum(reach - square * inverse, 0.0)
            guess = pl.reciprocal(reach, approx=True)
            reduced = ri * rj * (guess * (2.0 - reach * guess))
            closing = ((ui - uj) * dx + (vi - vj) * dy) * inverse
            m = overlap * reduced * (STIFFNESS - DAMPING * closing) * inverse
            sx = sx + m * dx
            sy = sy + m * dy
        forces[0, pl.ds(t, 1)] = jnp.sum(sx, axis=0, keepdims=True)
        forces[1, pl.ds(t, 1)] = jnp.sum(sy, axis=0, keepdims=True)
        return carry

    lax.fori_loop(0, slots // 2, contact, 0, unroll=UNROLL)

    landed(halo)
    sub8 = iota((8, width), 0)
    cnt[0:rows] = countf
    cnt[rows:] = jnp.where(sub8 < 4, halo_c[0], halo_c[1]).astype(f32)
    for c in range(2):
        wnd[c, 0:rows] = SURFACE_GAIN * wind[c]
        below, above = surf[2 + c, margin + rows : margin + rows + 8], surf[2 + c, margin - 8 : margin]
        wnd[c, rows:] = SURFACE_GAIN * jnp.where(sub8 < 4, below, above)
        surf[2 + c, margin : margin + rows] = wind[c]

    def fill(k, carry):
        wet = (cnt[...] > k.astype(f32)).astype(f32)
        for c in range(2):
            flow[c, k, 0:rows] = ocean[c, k] * wet[0:rows]
            flow[c, k, rows:] = jnp.where(sub8 < 4, halo_o[0, c, k], halo_o[1, c, k]) * wet[rows:]
        return carry

    lax.fori_loop(0, levels, fill, 0)

    lane72 = iota((ext, width), 1)
    inner = (lane72 % 8) < 4
    level72 = (lane72 // 8) % levels
    level_f = level72.astype(f32)

    def joined(part):
        return [
            jnp.concatenate([mid, jnp.where(sub8 < 4, corner[0, dc, part], corner[1, dc, part])], axis=0)
            for mid, dc in ((side[1, part], 2), (pack[part], 1), (side[0, part], 0))
        ]

    packed_aux, packed_flow = joined(1), joined(0)
    steer = []
    for which in range(2):
        mixed = [jnp.where(inner, p[which], p[which + 1]) for p in (packed_flow, packed_aux)]
        deep = jnp.where(level72 == 1, mixed[1], 0.0)
        for shift in (8, 16, 32):
            deep = deep + pltpu.roll(deep, shift, 1)
        wet = (deep > level_f).astype(f32)
        edge72[which, 0] = mixed[0] * wet
        edge72[which, 1] = wet
        edge72[which, 2] = jnp.where(level72 == 0, SURFACE_GAIN * mixed[1], 0.0)

    def substep(step, carry):
        def level(k, fluxes):
            after = jnp.minimum(k + 1, levels - 1)
            deep = cnt[...]
            wet = (deep > k.astype(f32)).astype(f32)
            wet_after = (deep > after.astype(f32)).astype(f32)
            h = 0.15 - 0.05 * k.astype(f32) / levels
            here = [flow[0, k], flow[1, k]]
            surface_on = jnp.where(k == 0, 1.0, 0.0)
            new_fluxes = []
            for c in range(2):
                x = here[c]
                at = 64 * c + 8 * k
                before = pltpu.roll(edge72[0, 0], 125 - at + jnp.where(at > 125, width, 0), 1)
                behind = pltpu.roll(edge72[1, 0], 123 - at, 1)
                left = jnp.where(lane72 == 0, before, pltpu.roll(x, 1, 1))
                right = jnp.where(lane72 == width - 1, behind, pltpu.roll(x, width - 1, 1))
                lap = pltpu.roll(x, 1, 0) + pltpu.roll(x, ext - 1, 0) + left + right - 4.0 * x
                flux = VERT_MIX * (flow[c, after] - x) * wet_after
                turn = CORIOLIS * here[1] if c == 0 else -CORIOLIS * here[0]
                new = x + h * lap + (flux - fluxes[c]) + turn + surface_on * wnd[c]
                flow[c, k] = new * wet
                new_fluxes.append(flux)
            return tuple(new_fluxes)

        nothing = jnp.zeros((ext, width), f32)
        lax.fori_loop(0, levels, level, (nothing, nothing))
        hp = 0.15 - 0.05 * level_f / levels
        turn_by = jnp.where(lane72 < 64, CORIOLIS, -CORIOLIS)
        for which in range(2):
            x, wet = edge72[which, 0], edge72[which, 1]
            lap = (
                pltpu.roll(x, 1, 0) + pltpu.roll(x, ext - 1, 0)
                + pltpu.roll(x, 1, 1) + pltpu.roll(x, width - 1, 1) - 4.0 * x
            )
            flux = VERT_MIX * (pltpu.roll(x, width - 8, 1) - x) * pltpu.roll(wet, width - 8, 1)
            flux = jnp.where(level72 < levels - 1, flux, 0.0)
            turn = turn_by * pltpu.roll(x, 64, 1)
            new = x + hp * lap + (flux - pltpu.roll(flux, 8, 1)) + turn + edge72[which, 2]
            edge72[which, 0] = new * wet
        return carry

    lax.fori_loop(0, OSTEPS, substep, 0)

    for c in range(2):
        late_s[c] = flow[c, 0, 0:rows]
    start(strips)
    for c in range(2):
        surf[c, margin : margin + rows] = late_s[c]

    def write(k, carry):
        for c in range(2):
            ocean_out[c, k] = flow[c, k, 0:rows]
        return carry

    lax.fori_loop(0, levels, write, 0)

    lax.fori_loop(slots // 2, slots, contact, 0, unroll=UNROLL)
    takes = (iota((blocks, slots), 0) == clist_v[0:1]) & (iota((blocks, slots), 1) < ccount[0, 0])
    takes = takes.astype(f32)
    push = [
        jnp.dot(takes, forces[c], precision=lax.Precision.HIGHEST, preferred_element_type=f32)
        for c in range(2)
    ]

    landed(strips)
    pieces = []
    for n in range(4):
        turned = surf[n].T
        high = turned.astype(jnp.bfloat16)
        low = (turned - high.astype(f32)).astype(jnp.bfloat16)
        pieces.append(jnp.concatenate([high, low], axis=1))
    table = jnp.concatenate(pieces, axis=0)
    first_cell = (row * rows - margin) * width
    sub = iota((2 * rows, 128), 0)
    columns = iota((width, 128), 0)
    for b in range(blocks):
        at = slice(128 * b, 128 * b + 128)
        q = cells[:, at] - first_cell
        hit_row = (sub == q // width).astype(f32).astype(jnp.bfloat16)
        found = jnp.dot(table, jnp.concatenate([hit_row, hit_row], axis=0), preferred_element_type=f32)
        hit_col = columns == q % width
        su, sv, wx, wy = [
            jnp.sum(jnp.where(hit_col, found[width * n : width * n + width], 0.0), axis=0, keepdims=True)
            for n in range(4)
        ]
        r = rad[:, at]
        u, v = vel[0:1, at], vel[1:2, at]
        area = math.pi * r * r
        ru, rv = su - u, sv - v
        speed = jnp.sqrt(ru * ru + rv * rv)
        fx = push[0][b : b + 1] + area * (WATER_DRAG * speed * ru + AIR_GAIN * wx)
        fy = push[1][b : b + 1] + area * (WATER_DRAG * speed * rv + AIR_GAIN * wy)
        per_mass = ICE_STEP / mass[:, at]
        nu, nv = u + fx * per_mass, v + fy * per_mass
        floe_out[0:1, at] = pos[0:1, at] + ICE_STEP * nu
        floe_out[1:2, at] = pos[1:2, at] + ICE_STEP * nv
        floe_out[2:3, at] = nu
        floe_out[3:4, at] = nv

    def gather_late(w, carry):
        index = jnp.broadcast_to(mindex[pl.ds(w, 1)], (8, 128))
        block, lanes = index // 128, index % 128
        total = jnp.zeros((8, 128), f32)
        for b in range(blocks):
            values = floe_out[:, 128 * b : 128 * b + 128]
            values = jnp.concatenate([values, values], axis=0)
            total = jnp.where(block == b, lane_gather(values, lanes), total)
        next_s[w] = jnp.where(lane8 < mcount[0, w], total, 0.0)
        return carry

    lax.fori_loop(0, 8, gather_late, 0)
    start(late)
    landed(early)
    for w in range(8):
        arrive_out[w, 6:38] = early_r[w, 0:32]
        arrive_out[w, 4:6] = early_r[w, 32:34]
    landed(late)
    for w in range(8):
        arrive_out[w, 0:4] = next_r[w, 0:4]
    for copies in (halo, records, early, strips, late):
        sent(copies)


def shards(
    ocean_velocity, wind_stress, level_counts, floe_position, floe_velocity, floe_radius, floe_mass,
    floe_polygon, remap_cells, contact_count, contact_list, move_index, move_count,
):
    levels, rows, width = ocean_velocity.shape[1:]
    floes = floe_position.shape[-1]
    blocks = floes // 128
    slots = contact_list.shape[-1]
    ext = rows + 8
    lists = contact_list[0, 0]
    vmem = pl.BlockSpec(memory_space=pltpu.VMEM)
    smem = pl.BlockSpec(memory_space=pltpu.SMEM)
    fields = 2 + floe_polygon.shape[2] + 4
    flow, floe, arrivals = pl.pallas_call(
        kernel,
        out_shape=(
            jax.ShapeDtypeStruct(ocean_velocity.shape, f32),
            jax.ShapeDtypeStruct((4, floes), f32),
            jax.ShapeDtypeStruct((8, fields, 128), f32),
        ),
        in_specs=[pl.BlockSpec(memory_space=pltpu.HBM)] * 9 + [smem, smem, vmem, vmem, smem],
        out_specs=(vmem, vmem, vmem),
        scratch_shapes=[
            pltpu.VMEM((2, levels, ext, width), f32),
            pltpu.VMEM((ext, width), f32),
            pltpu.VMEM((2, ext, width), f32),
            pltpu.VMEM((2, 2, levels, 8, width), f32),
            pltpu.VMEM((2, 8, width), jnp.int32),
            pltpu.VMEM((2, rows, width), f32),
            pltpu.VMEM((2, 2, rows, width), f32),
            pltpu.VMEM((2, 3, 2, 8, width), f32),
            pltpu.VMEM((2, 3, ext, width), f32),
            pltpu.VMEM((blocks, 8, 128), f32),
            pltpu.VMEM((8 * GHOST, 8, 128), f32),
            pltpu.VMEM((blocks + 8 * GHOST, 128, 8), f32),
            pltpu.VMEM((2, slots, 128), f32),
            pltpu.VMEM((4, 2 * rows, width), f32),
            pltpu.VMEM((2, rows, width), f32),
            pltpu.VMEM((8, 40, 128), f32),
            pltpu.VMEM((8, 40, 128), f32),
            pltpu.VMEM((8, 8, 128), f32),
            pltpu.VMEM((8, 8, 128), f32),
            pltpu.VMEM(ocean_velocity.shape, f32),
            pltpu.VMEM(wind_stress.shape, f32),
            pltpu.VMEM(level_counts.shape, jnp.int32),
            pltpu.VMEM((2, floes), f32),
            pltpu.VMEM((2, floes), f32),
            pltpu.VMEM((1, floes), f32),
            pltpu.VMEM((1, floes), f32),
            pltpu.VMEM(floe_polygon.shape[2:], f32),
            pltpu.VMEM((1, floes), jnp.int32),
            pltpu.SemaphoreType.DMA((40,)),
            pltpu.SemaphoreType.DMA((40,)),
            pltpu.SemaphoreType.DMA((9,)),
        ],
        compiler_params=pltpu.CompilerParams(
            collective_id=0, has_side_effects=True, vmem_limit_bytes=60 * 1024 * 1024
        ),
    )(
        ocean_velocity, wind_stress, level_counts, floe_position[0, 0], floe_velocity[0, 0],
        floe_radius[0], floe_mass[0], floe_polygon[0, 0], remap_cells[0], contact_count,
        lists, lists, move_index[0, 0], move_count[0],
    )
    return (flow, floe[None, None], arrivals[None, None])


def solution(mesh):
    tile = P("gx", ("sec", "gy"))
    return jax.shard_map(
        shards,
        mesh=mesh,
        in_specs=(
            P(None, None, "gx", ("sec", "gy")),
            P(None, "gx", ("sec", "gy")),
            tile, tile, tile, tile, tile, tile, tile, tile, tile, tile, tile,
        ),
        out_specs=(P(None, None, "gx", ("sec", "gy")), tile, tile),
        check_vma=False,
    )
```

```python
import functools
import math

import jax
import jax.numpy as jnp
from jax import lax
from jax.experimental import pallas as pl
from jax.experimental.pallas import tpu as pltpu
from jax.sharding import PartitionSpec as P

OSTEPS = 4
GHOST = 4
SOFTEN = 0.1
STIFFNESS = 0.1
DAMPING = 0.05
VERT_MIX = 0.15
CORIOLIS = 0.1
SURFACE_GAIN = 0.25
WATER_DRAG = 0.1
AIR_GAIN = 0.2
ICE_STEP = 0.5
PLACES = (0, 1, 2, 3, 5, 6, 7, 8)
UP, LEFT, RIGHT, DOWN = 1, 3, 4, 6
MESH = pl.DeviceIdType.MESH
f32 = jnp.float32
UNROLL = 4


def lane_gather(values, lanes):
    return jnp.take_along_axis(values, lanes, axis=1, mode="promise_in_bounds")


def iota(shape, dim):
    return lax.broadcasted_iota(jnp.int32, shape, dim)


def kernel(
    ocean_h, wind_h, counts_h, pos_h, vel_h, rad_h, mass_h, poly_h, cells_h,
    ccount, clist, clist_v, mindex, mcount,
    ocean_out, floe_out, arrive_out,
    flow, cnt, wnd, halo_o, halo_c, pack, side, corner, edge72, own, gh, cols, forces,
    surf, late_s, early_s, early_r, next_s, next_r,
    ocean, wind, counts, pos, vel, rad, mass, poly, cells,
    sem_s, sem_r, sem_i,
):
    loads = [
        pltpu.make_async_copy(src, dst, sem_i.at[n])
        for n, (src, dst) in enumerate((
            (ocean_h, ocean), (wind_h, wind), (counts_h, counts), (pos_h, pos), (vel_h, vel),
            (rad_h, rad), (poly_h, poly), (mass_h, mass), (cells_h, cells),
        ))
    ]
    for load in loads:
        load.start()
    levels, rows, width = ocean.shape[1], ocean.shape[2], ocean.shape[3]
    floes = pos.shape[1]
    blocks = floes // 128
    ext = rows + 8
    margin = rows // 2
    slots = clist.shape[1]
    n_gy = lax.axis_size("gy")
    n_rows, n_cols = lax.axis_size("gx"), lax.axis_size("sec") * n_gy
    row = lax.axis_index("gx")
    col = lax.axis_index("sec") * n_gy + lax.axis_index("gy")

    there, ids = [], []
    for way in range(8):
        dr, dc = PLACES[way] // 3 - 1, PLACES[way] % 3 - 1
        r, c = row + dr, col + dc
        there.append((r >= 0) & (r < n_rows) & (c >= 0) & (c < n_cols))
        ids.append((c // n_gy, r, c % n_gy))

    def copy(src, dst, number, way):
        return pltpu.make_async_remote_copy(
            src_ref=src, dst_ref=dst, send_sem=sem_s.at[number], recv_sem=sem_r.at[number],
            device_id=ids[way], device_id_type=MESH,
        )

    for ref in (halo_o, halo_c, side, corner, gh, early_r, next_r):
        ref[...] = jnp.zeros_like(ref)
    surf[:, 0:margin] = jnp.zeros((4, margin, width), f32)
    surf[:, margin + rows :] = jnp.zeros((4, margin, width), f32)

    barrier = pltpu.get_barrier_semaphore()
    for way in range(8):
        @pl.when(there[way])
        def _():
            pl.semaphore_signal(barrier, inc=1, device_id=ids[way], device_id_type=MESH)

    for load in loads[:6]:
        load.wait()
    for b in range(blocks):
        at = slice(128 * b, 128 * b + 128)
        own[b, 0:2] = pos[:, at]
        own[b, 2:4] = vel[:, at]
        own[b, 4:5] = rad[:, at]
        own[b, 5:8] = jnp.zeros((3, 128), f32)
    lane = iota((rows, width), 1)
    group = lane // 8
    pack_flow = jnp.zeros((rows, width), f32)
    for c in range(2):
        for k in range(levels):
            n = c * levels + k
            pack_flow = jnp.where(group == n, pltpu.roll(ocean[c, k], (8 * n + 4) % width, 1), pack_flow)
    pack[0] = pack_flow
    countf = counts[...].astype(f32)
    aux = jnp.zeros((rows, width), f32)
    for c in range(2):
        n = c * levels
        aux = jnp.where(group == n, pltpu.roll(wind[c], (8 * n + 4) % width, 1), aux)
        aux = jnp.where(group == n + 1, pltpu.roll(countf, (8 * n + 12) % width, 1), aux)
    pack[1] = aux

    pl.semaphore_wait(barrier, sum(t.astype(jnp.int32) for t in there))

    halo = []
    strips = []
    for way in range(8):
        dr, dc = PLACES[way] // 3 - 1, PLACES[way] % 3 - 1
        first = 0 if dr < 0 else rows - 8
        if dr == 0:
            halo.append((way, copy(pack, side.at[(dc + 1) // 2], way, way)))
        else:
            part = pl.ds(first, 8)
            d = (dr + 1) // 2
            halo.append((way, copy(pack.at[:, part], corner.at[d, dc + 1], way, way)))
            if dc == 0:
                halo.append((way, copy(ocean.at[:, :, part], halo_o.at[d], 8 + d, way)))
                halo.append((way, copy(counts.at[part], halo_c.at[d], 10 + d, way)))
                src = pl.ds(0 if dr < 0 else rows - margin, margin)
                dst = pl.ds(rows + margin if dr < 0 else 0, margin)
                halo.append((way, copy(wind.at[:, src], surf.at[2:4, dst], 12 + d, way)))
                strips.append((way, copy(late_s.at[:, src], surf.at[0:2, dst], 14 + d, way)))
    records = [(w, copy(own.at[0:GHOST], gh.at[pl.ds((7 - w) * GHOST, GHOST)], 16 + w, w)) for w in range(8)]
    early = [(w, copy(early_s.at[w], early_r.at[w], 24 + w, w)) for w in range(8)]
    late = [(w, copy(next_s.at[w], next_r.at[w], 32 + w, w)) for w in range(8)]

    def start(copies):
        for way, c in copies:
            pl.when(there[way])(c.start)

    def landed(copies):
        for way, c in copies:
            pl.when(there[7 - way])(c.wait_recv)

    def sent(copies):
        for way, c in copies:
            pl.when(there[way])(c.wait_send)

    start(records)
    start(halo)

    for load in loads[6:]:
        load.wait()
    lane8 = iota((8, 128), 1)

    def gather_early(w, carry):
        index = jnp.broadcast_to(mindex[pl.ds(w, 1)], (8, 128))
        block, lanes = index // 128, index % 128
        valid = lane8 < mcount[0, w]
        groups = [jnp.zeros((8, 128), f32) for _ in range(5)]
        for b in range(blocks):
            at = slice(128 * b, 128 * b + 128)
            hit = block == b
            for g in range(4):
                groups[g] = jnp.where(hit, lane_gather(poly[8 * g : 8 * g + 8, at], lanes), groups[g])
            rm = jnp.concatenate([rad[:, at], mass[:, at], jnp.zeros((6, 128), f32)], axis=0)
            groups[4] = jnp.where(hit, lane_gather(rm, lanes), groups[4])
        for g in range(5):
            early_s[w, 8 * g : 8 * g + 8] = jnp.where(valid, groups[g], 0.0)
        return carry

    lax.fori_loop(0, 8, gather_early, 0)
    start(early)

    def own_cols(b, carry):
        cols[b] = own[b].T
        return carry

    lax.fori_loop(0, blocks, own_cols, 0, unroll=8)

    landed(records)

    def ghost_cols(b, carry):
        cols[blocks + b] = gh[b].T
        return carry

    lax.fori_loop(0, 8 * GHOST, ghost_cols, 0, unroll=8)

    def contact(t, carry):
        a, s, c = clist[0, t], clist[1, t], clist[2, t]
        neighbour = s - (s > 4).astype(jnp.int32)
        partner = jnp.where(s == 4, c, blocks + neighbour * GHOST + c)
        partner = jnp.clip(partner, 0, blocks + 8 * GHOST - 1)
        mine = own[a]
        other = cols[partner]
        step = 64
        xi, yi, ui, vi, ri = [jnp.broadcast_to(mine[f : f + 1], (step, 128)) for f in range(5)]
        sx = jnp.zeros((step, 128), f32)
        sy = jnp.zeros((step, 128), f32)
        for q in range(0, 128, step):
            xj, yj, uj, vj, rj = [
                jnp.broadcast_to(other[q : q + step, f : f + 1], (step, 128)) for f in range(5)
            ]
            dx, dy = xi - xj, yi - yj
            square = dx * dx + dy * dy + SOFTEN * SOFTEN
            inverse = lax.rsqrt(square)
            reach = ri + rj
            overlap = jnp.maximum(reach - square * inverse, 0.0)
            guess = pl.reciprocal(reach, approx=True)
            reduced = ri * rj * (guess * (2.0 - reach * guess))
            closing = ((ui - uj) * dx + (vi - vj) * dy) * inverse
            m = overlap * reduced * (STIFFNESS - DAMPING * closing) * inverse
            sx = sx + m * dx
            sy = sy + m * dy
        forces[0, pl.ds(t, 1)] = jnp.sum(sx, axis=0, keepdims=True)
        forces[1, pl.ds(t, 1)] = jnp.sum(sy, axis=0, keepdims=True)
        return carry

    lax.fori_loop(0, slots // 2, contact, 0, unroll=UNROLL)

    landed(halo)
    sub8 = iota((8, width), 0)
    cnt[0:rows] = countf
    cnt[rows:] = jnp.where(sub8 < 4, halo_c[0], halo_c[1]).astype(f32)
    for c in range(2):
        wnd[c, 0:rows] = SURFACE_GAIN * wind[c]
        below, above = surf[2 + c, margin + rows : margin + rows + 8], surf[2 + c, margin - 8 : margin]
        wnd[c, rows:] = SURFACE_GAIN * jnp.where(sub8 < 4, below, above)
        surf[2 + c, margin : margin + rows] = wind[c]

    def fill(k, carry):
        wet = (cnt[...] > k.astype(f32)).astype(f32)
        for c in range(2):
            flow[c, k, 0:rows] = ocean[c, k] * wet[0:rows]
            flow[c, k, rows:] = jnp.where(sub8 < 4, halo_o[0, c, k], halo_o[1, c, k]) * wet[rows:]
        return carry

    lax.fori_loop(0, levels, fill, 0)

    lane72 = iota((ext, width), 1)
    inner = (lane72 % 8) < 4
    level72 = (lane72 // 8) % levels
    level_f = level72.astype(f32)

    def joined(part):
        return [
            jnp.concatenate([mid, jnp.where(sub8 < 4, corner[0, dc, part], corner[1, dc, part])], axis=0)
            for mid, dc in ((side[1, part], 2), (pack[part], 1), (side[0, part], 0))
        ]

    packed_aux, packed_flow = joined(1), joined(0)
    steer = []
    for which in range(2):
        mixed = [jnp.where(inner, p[which], p[which + 1]) for p in (packed_flow, packed_aux)]
        deep = jnp.where(level72 == 1, mixed[1], 0.0)
        for shift in (8, 16, 32):
            deep = deep + pltpu.roll(deep, shift, 1)
        wet = (deep > level_f).astype(f32)
        edge72[which, 0] = mixed[0] * wet
        edge72[which, 1] = wet
        edge72[which, 2] = jnp.where(level72 == 0, SURFACE_GAIN * mixed[1], 0.0)

    def substep(step, carry):
        def level(k, fluxes):
            after = jnp.minimum(k + 1, levels - 1)
            deep = cnt[...]
            wet = (deep > k.astype(f32)).astype(f32)
            wet_after = (deep > after.astype(f32)).astype(f32)
            h = 0.15 - 0.05 * k.astype(f32) / levels
            here = [flow[0, k], flow[1, k]]
            surface_on = jnp.where(k == 0, 1.0, 0.0)
            new_fluxes = []
            for c in range(2):
                x = here[c]
                at = 64 * c + 8 * k
                before = pltpu.roll(edge72[0, 0], 125 - at + jnp.where(at > 125, width, 0), 1)
                behind = pltpu.roll(edge72[1, 0], 123 - at, 1)
                left = jnp.where(lane72 == 0, before, pltpu.roll(x, 1, 1))
                right = jnp.where(lane72 == width - 1, behind, pltpu.roll(x, width - 1, 1))
                lap = pltpu.roll(x, 1, 0) + pltpu.roll(x, ext - 1, 0) + left + right - 4.0 * x
                flux = VERT_MIX * (flow[c, after] - x) * wet_after
                turn = CORIOLIS * here[1] if c == 0 else -CORIOLIS * here[0]
                new = x + h * lap + (flux - fluxes[c]) + turn + surface_on * wnd[c]
                flow[c, k] = new * wet
                new_fluxes.append(flux)
            return tuple(new_fluxes)

        nothing = jnp.zeros((ext, width), f32)
        lax.fori_loop(0, levels, level, (nothing, nothing), unroll=2)
        hp = 0.15 - 0.05 * level_f / levels
        turn_by = jnp.where(lane72 < 64, CORIOLIS, -CORIOLIS)
        for which in range(2):
            x, wet = edge72[which, 0], edge72[which, 1]
            lap = (
                pltpu.roll(x, 1, 0) + pltpu.roll(x, ext - 1, 0)
                + pltpu.roll(x, 1, 1) + pltpu.roll(x, width - 1, 1) - 4.0 * x
            )
            flux = VERT_MIX * (pltpu.roll(x, width - 8, 1) - x) * pltpu.roll(wet, width - 8, 1)
            flux = jnp.where(level72 < levels - 1, flux, 0.0)
            turn = turn_by * pltpu.roll(x, 64, 1)
            new = x + hp * lap + (flux - pltpu.roll(flux, 8, 1)) + turn + edge72[which, 2]
            edge72[which, 0] = new * wet
        return carry

    lax.fori_loop(0, OSTEPS, substep, 0)

    for c in range(2):
        late_s[c] = flow[c, 0, 0:rows]
    start(strips)
    for c in range(2):
        surf[c, margin : margin + rows] = late_s[c]

    store = pltpu.make_async_copy(flow.at[:, :, pl.ds(0, rows)], ocean_out, sem_i.at[9])
    store.start()

    lax.fori_loop(slots // 2, slots, contact, 0, unroll=UNROLL)
    takes = (iota((blocks, slots), 0) == clist_v[0:1]) & (iota((blocks, slots), 1) < ccount[0, 0])
    takes = takes.astype(f32)
    push = [
        jnp.dot(takes, forces[c], precision=lax.Precision.HIGHEST, preferred_element_type=f32)
        for c in range(2)
    ]

    landed(strips)
    pieces = []
    for n in range(4):
        turned = surf[n].T
        high = turned.astype(jnp.bfloat16)
        low = (turned - high.astype(f32)).astype(jnp.bfloat16)
        pieces.append(jnp.concatenate([high, low], axis=1))
    table = jnp.concatenate(pieces, axis=0)
    first_cell = (row * rows - margin) * width
    sub = iota((2 * rows, 128), 0)
    columns = iota((width, 128), 0)
    for b in range(blocks):
        at = slice(128 * b, 128 * b + 128)
        q = cells[:, at] - first_cell
        hit_row = (sub == q // width).astype(f32).astype(jnp.bfloat16)
        found = jnp.dot(table, jnp.concatenate([hit_row, hit_row], axis=0), preferred_element_type=f32)
        hit_col = columns == q % width
        su, sv, wx, wy = [
            jnp.sum(jnp.where(hit_col, found[width * n : width * n + width], 0.0), axis=0, keepdims=True)
            for n in range(4)
        ]
        r = rad[:, at]
        u, v = vel[0:1, at], vel[1:2, at]
        area = math.pi * r * r
        ru, rv = su - u, sv - v
        speed = jnp.sqrt(ru * ru + rv * rv)
        fx = push[0][b : b + 1] + area * (WATER_DRAG * speed * ru + AIR_GAIN * wx)
        fy = push[1][b : b + 1] + area * (WATER_DRAG * speed * rv + AIR_GAIN * wy)
        per_mass = ICE_STEP / mass[:, at]
        nu, nv = u + fx * per_mass, v + fy * per_mass
        floe_out[0:1, at] = pos[0:1, at] + ICE_STEP * nu
        floe_out[1:2, at] = pos[1:2, at] + ICE_STEP * nv
        floe_out[2:3, at] = nu
        floe_out[3:4, at] = nv

    def gather_late(w, carry):
        index = jnp.broadcast_to(mindex[pl.ds(w, 1)], (8, 128))
        block, lanes = index // 128, index % 128
        total = jnp.zeros((8, 128), f32)
        for b in range(blocks):
            values = floe_out[:, 128 * b : 128 * b + 128]
            values = jnp.concatenate([values, values], axis=0)
            total = jnp.where(block == b, lane_gather(values, lanes), total)
        next_s[w] = jnp.where(lane8 < mcount[0, w], total, 0.0)
        return carry

    lax.fori_loop(0, 8, gather_late, 0)
    start(late)
    landed(early)
    for w in range(8):
        arrive_out[w, 6:38] = early_r[w, 0:32]
        arrive_out[w, 4:6] = early_r[w, 32:34]
    landed(late)
    for w in range(8):
        arrive_out[w, 0:4] = next_r[w, 0:4]
    for copies in (halo, records, early, strips, late):
        sent(copies)
    store.wait()


def shards(
    ocean_velocity, wind_stress, level_counts, floe_position, floe_velocity, floe_radius, floe_mass,
    floe_polygon, remap_cells, contact_count, contact_list, move_index, move_count,
):
    levels, rows, width = ocean_velocity.shape[1:]
    floes = floe_position.shape[-1]
    blocks = floes // 128
    slots = contact_list.shape[-1]
    ext = rows + 8
    lists = contact_list[0, 0]
    vmem = pl.BlockSpec(memory_space=pltpu.VMEM)
    smem = pl.BlockSpec(memory_space=pltpu.SMEM)
    fields = 2 + floe_polygon.shape[2] + 4
    flow, floe, arrivals = pl.pallas_call(
        kernel,
        out_shape=(
            jax.ShapeDtypeStruct(ocean_velocity.shape, f32),
            jax.ShapeDtypeStruct((4, floes), f32),
            jax.ShapeDtypeStruct((8, fields, 128), f32),
        ),
        in_specs=[pl.BlockSpec(memory_space=pltpu.HBM)] * 9 + [smem, smem, vmem, vmem, smem],
        out_specs=(pl.BlockSpec(memory_space=pltpu.HBM), vmem, vmem),
        scratch_shapes=[
            pltpu.VMEM((2, levels, ext, width), f32),
            pltpu.VMEM((ext, width), f32),
            pltpu.VMEM((2, ext, width), f32),
            pltpu.VMEM((2, 2, levels, 8, width), f32),
            pltpu.VMEM((2, 8, width), jnp.int32),
            pltpu.VMEM((2, rows, width), f32),
            pltpu.VMEM((2, 2, rows, width), f32),
            pltpu.VMEM((2, 3, 2, 8, width), f32),
            pltpu.VMEM((2, 3, ext, width), f32),
            pltpu.VMEM((blocks, 8, 128), f32),
            pltpu.VMEM((8 * GHOST, 8, 128), f32),
            pltpu.VMEM((blocks + 8 * GHOST, 128, 8), f32),
            pltpu.VMEM((2, slots, 128), f32),
            pltpu.VMEM((4, 2 * rows, width), f32),
            pltpu.VMEM((2, rows, width), f32),
            pltpu.VMEM((8, 40, 128), f32),
            pltpu.VMEM((8, 40, 128), f32),
            pltpu.VMEM((8, 8, 128), f32),
            pltpu.VMEM((8, 8, 128), f32),
            pltpu.VMEM(ocean_velocity.shape, f32),
            pltpu.VMEM(wind_stress.shape, f32),
            pltpu.VMEM(level_counts.shape, jnp.int32),
            pltpu.VMEM((2, floes), f32),
            pltpu.VMEM((2, floes), f32),
            pltpu.VMEM((1, floes), f32),
            pltpu.VMEM((1, floes), f32),
            pltpu.VMEM(floe_polygon.shape[2:], f32),
            pltpu.VMEM((1, floes), jnp.int32),
            pltpu.SemaphoreType.DMA((40,)),
            pltpu.SemaphoreType.DMA((40,)),
            pltpu.SemaphoreType.DMA((10,)),
        ],
        compiler_params=pltpu.CompilerParams(
            collective_id=0, has_side_effects=True, vmem_limit_bytes=60 * 1024 * 1024
        ),
    )(
        ocean_velocity, wind_stress, level_counts, floe_position[0, 0], floe_velocity[0, 0],
        floe_radius[0], floe_mass[0], floe_polygon[0, 0], remap_cells[0], contact_count,
        lists, lists, move_index[0, 0], move_count[0],
    )
    return (flow, floe[None, None], arrivals[None, None])


def solution(mesh):
    tile = P("gx", ("sec", "gy"))
    return jax.shard_map(
        shards,
        mesh=mesh,
        in_specs=(
            P(None, None, "gx", ("sec", "gy")),
            P(None, "gx", ("sec", "gy")),
            tile, tile, tile, tile, tile, tile, tile, tile, tile, tile, tile,
        ),
        out_specs=(P(None, None, "gx", ("sec", "gy")), tile, tile),
        check_vma=False,
    )
```
